32 devices in a mesh: energy: 2 (over x), chain: 16 (over z, y, core).
Axes of the slice: x: 2, y: 2, z: 4, core: 2. Of those that a mesh axis runs over, the one named last changes fastest.
Arguments:
- lower: bfloat16 [32, 2, 256, 256], P(('energy', 'chain')), parts along dimension 0, may hold values from -0.125 to 0.125
- upper: bfloat16 [32, 2, 256, 256], P(('energy', 'chain')), parts along dimension 0, may hold values from -0.125 to 0.125
- right_side: bfloat16 [32, 2, 256, 256], P(('energy', 'chain')), parts along dimension 0, may hold values from -6 to 6
Outputs:
- reduced_rhs: bfloat16 [32, 2, 256, 256], P(('energy', 'chain')), parts along dimension 0
The draws below stay inside these ranges and needn't reach their ends.
There are 2 independent parts, one for each index of `energy`. The reference program is written for one: setup_inputs(seed, part) draws one part's arguments, and reference() takes and returns one part's arrays. A program takes and returns all parts, laid end to end along the dimension named above; each array names one. Nothing has to cross between parts.
All inputs are finite; a program needn't handle non-finite values.
Results may differ from the reference program's by a relative error of at most 0.011.
Values may be sent and summed in bfloat16 or wider, within the bound.
No kernel may reach another device: no remote copies, remote signals or barrier semaphores. Data moves between devices by JAX's collectives and lax.ppermute only.
A program may use at most 64 MiB of HBM per device.

```python
import jax
import jax.numpy as jnp

M = 256
COLS = 256
SECTIONS = 3
NS_STEPS = 2
ROWS = 16


def block_scale(stream_key, shape, shards, least, high):
    def one(axis_at, parts):
        steps = jax.random.uniform(jax.random.fold_in(jax.random.fold_in(stream_key, 6), axis_at), (parts,), jnp.float32, least / len(shards), high / len(shards))
        return jnp.repeat(jnp.exp(steps), shape[axis_at] // parts).reshape((-1,) + (1,) * (len(shape) - axis_at - 1))

    loudness = one(*shards[0])
    for cut in shards[1:]:
        loudness = loudness * one(*cut)
    return loudness


def scatter_about(key, extent, spread, most, split=(), kind=jnp.bfloat16):
    level = block_scale(key, extent, split, -0.22, 0.18) if split else 1.0
    entries = jax.random.normal(key, extent, jnp.float32) * spread * level
    return jnp.minimum(jnp.maximum(entries, -most), most).astype(kind)


def setup_inputs(seed: int = 0, part: int = 0) -> dict:
    arg_keys = jax.random.split(jax.random.key(seed), 4)
    part_keys = jax.random.split(jax.random.fold_in(arg_keys[3], part), 4)
    return {
        "lower": scatter_about(part_keys[0], (ROWS, 2, M, M), (7 * M) ** -0.5, 0.125, ((0, 16),)),
        "upper": scatter_about(part_keys[1], (ROWS, 2, M, M), (7 * M) ** -0.5, 0.125, ((0, 16),)),
        "right_side": scatter_about(part_keys[2], (ROWS, 2, M, COLS), 1.0, 6.0, ((0, 16),)),
    }


def complex_product(left_block, right_block):
    left_f = left_block.astype(jnp.float32)
    right_f = right_block.astype(jnp.float32)
    real_part = jnp.einsum("nij,njk->nik", left_f[:, 0], right_f[:, 0]) - jnp.einsum("nij,njk->nik", left_f[:, 1], right_f[:, 1])
    imag_part = jnp.einsum("nij,njk->nik", left_f[:, 0], right_f[:, 1]) + jnp.einsum("nij,njk->nik", left_f[:, 1], right_f[:, 0])
    return jnp.stack([real_part, imag_part], axis=1)


def from_below(values, reach):
    padding = jnp.zeros_like(values[:reach])
    return jnp.concatenate([padding, values[:-reach]], axis=0)


def from_above(values, reach):
    padding = jnp.zeros_like(values[:reach])
    return jnp.concatenate([values[reach:], padding], axis=0)


def approx_inverse(diagonal_new, identity_block):
    diagonal_low = diagonal_new.astype(jnp.bfloat16)
    approx = (2.0 * identity_block - diagonal_new).astype(jnp.bfloat16)
    for repeat in range(NS_STEPS):
        correction = (2.0 * identity_block - complex_product(diagonal_low, approx)).astype(jnp.bfloat16)
        approx = complex_product(approx, correction).astype(jnp.bfloat16)
    return approx


def reference(lower, upper, right_side):
    unit_matrix = jnp.eye(M, dtype=jnp.float32)
    identity_block = jnp.stack([unit_matrix, jnp.zeros_like(unit_matrix)])[None]
    lower_block = lower
    upper_block = upper
    current = right_side
    for number in range(SECTIONS):
        reach = 2 ** number
        final = number == SECTIONS - 1
        below_lower = from_below(lower_block, reach)
        below_upper = from_below(upper_block, reach)
        below_rhs = from_below(current, reach)
        above_lower = from_above(lower_block, reach)
        above_upper = from_above(upper_block, reach)
        above_rhs = from_above(current, reach)
        diagonal_new = identity_block - complex_product(lower_block, below_upper) - complex_product(upper_block, above_lower)
        inverse = approx_inverse(diagonal_new, identity_block)
        rhs_new = (current - complex_product(lower_block, below_rhs) - complex_product(upper_block, above_rhs)).astype(jnp.bfloat16)
        if not final:
            lower_raw = (-complex_product(lower_block, below_lower)).astype(jnp.bfloat16)
            upper_raw = (-complex_product(upper_block, above_upper)).astype(jnp.bfloat16)
            lower_block = complex_product(inverse, lower_raw).astype(jnp.bfloat16)
            upper_block = complex_product(inverse, upper_raw).astype(jnp.bfloat16)
        current = complex_product(inverse, rhs_new).astype(jnp.bfloat16)
    return current
```

```python
import functools

import jax
import jax.numpy as jnp
from jax import lax
from jax.experimental import pallas as pl
from jax.experimental.pallas import tpu as pltpu
from jax.sharding import PartitionSpec as P

SECTIONS = 3
GROUP = 4
LOW, UPP = 0, 1


def wide(block):
    real, imag = block[0], block[1]
    return jnp.concatenate(
        [jnp.concatenate([real, -imag], axis=1), jnp.concatenate([imag, real], axis=1)], axis=0
    )


def tall(block):
    return block.reshape(block.shape[0] * block.shape[1], block.shape[2])


def product(left, right):
    return jnp.dot(left, right, preferred_element_type=jnp.float32)


def low(value):
    return value.astype(jnp.bfloat16)


def parts(stacked, order):
    return stacked.reshape(2, order, stacked.shape[-1])


def inverse_less_one(coupling, order):
    first = low(coupling)
    first_wide = wide(parts(first, order))
    second = product(first_wide, first)
    second_low = low(second)
    pair = product(wide(parts(second_low, order)), jnp.concatenate([second_low, first], axis=1))
    fourth = low(pair[:, :order])
    short = coupling + second + pair[:, order:]
    whole = short + fourth.astype(jnp.float32) + product(
        wide(parts(low(short), order)), fourth
    )
    return low(whole)


def couplings_kernel(flags, own_a, own_b, near, far_a, far_b, new, spread, own_out):
    order = near.shape[2]
    side = flags[0]
    middle = flags[1]

    @pl.when(middle == 1)
    def _():
        own_out[...] = own_b[...]

    @pl.when(middle == 0)
    def _():
        own_out[...] = own_a[...]

    near_lead = wide(own_out[side])
    far_lead = wide(own_out[1 - side])
    far_cross = jnp.where(middle == 1, far_a[side], far_b[side])
    far_same = jnp.where(middle == 1, far_a[1 - side], far_b[1 - side])
    coupling = product(near_lead, tall(near[1 - side])) + product(far_lead, tall(far_cross))
    spread_low = inverse_less_one(coupling, order)
    spread[...] = parts(spread_low, order)
    spread_wide = wide(parts(spread_low, order))
    for place, lead, same in ((side, near_lead, near[side]), (1 - side, far_lead, far_same)):
        raw = -product(lead, tall(same))
        new[place] = parts(low(raw + product(spread_wide, low(raw))), order)


def injections_kernel(flags, own_lu, spread, own_a, own_b, near, far_a, far_b, new):
    order = near.shape[1]
    side = flags[0]
    middle = flags[1]
    own = tall(jnp.where(middle == 1, own_b[...], own_a[...]))
    far = tall(jnp.where(middle == 1, far_a[...], far_b[...]))
    raw = (
        own.astype(jnp.float32)
        - product(wide(own_lu[side]), tall(near[...]))
        - product(wide(own_lu[1 - side]), far)
    )
    new[...] = parts(low(raw + product(wide(spread[...]), low(raw))), order)


def later_couplings_kernel(own, below, above, new, spread):
    order = own.shape[2]
    lower_wide = wide(own[LOW])
    upper_wide = wide(own[UPP])
    coupling = product(lower_wide, tall(below[UPP])) + product(upper_wide, tall(above[LOW]))
    spread_low = inverse_less_one(coupling, order)
    spread[...] = parts(spread_low, order)
    spread_wide = wide(parts(spread_low, order))
    for place, lead, same in ((LOW, lower_wide, below), (UPP, upper_wide, above)):
        raw = -product(lead, tall(same[place]))
        new[place] = parts(low(raw + product(spread_wide, low(raw))), order)


def last_couplings_kernel(own, below_upper, above_lower, spread):
    order = own.shape[2]
    coupling = product(wide(own[LOW]), tall(below_upper[...])) + product(
        wide(own[UPP]), tall(above_lower[...])
    )
    spread[...] = parts(inverse_less_one(coupling, order), order)


def later_injections_kernel(own_lu, spread, own, below, above, new):
    order = own.shape[1]
    raw = (
        tall(own[...]).astype(jnp.float32)
        - product(wide(own_lu[LOW]), tall(below[...]))
        - product(wide(own_lu[UPP]), tall(above[...]))
    )
    new[...] = parts(low(raw + product(wide(spread[...]), low(raw))), order)


def run(kernel, products, outs, *operands, scalars=0):
    order = operands[-1].shape[-1]
    count = len(operands)
    bytes_in = sum(o.size * o.dtype.itemsize for o in operands)
    return pl.pallas_call(
        kernel,
        out_shape=[jax.ShapeDtypeStruct(s, jnp.bfloat16) for s in outs],
        in_specs=[pl.BlockSpec(memory_space=pltpu.SMEM)] * scalars
        + [pl.BlockSpec(memory_space=pltpu.VMEM)] * (count - scalars),
        out_specs=[pl.BlockSpec(memory_space=pltpu.VMEM)] * len(outs),
        compiler_params=pltpu.CompilerParams(vmem_limit_bytes=24 * 1024 * 1024),
        cost_estimate=pl.CostEstimate(
            flops=products * 8 * order**3, bytes_accessed=bytes_in, transcendentals=0
        ),
    )(*operands)


def local(length, lower, upper, right_side):
    order = lower.shape[2]
    block = (2, order, order)
    pair = (2,) + block
    place = lax.axis_index("chain")
    spot = place % GROUP
    side = jnp.where(spot < GROUP // 2, UPP, LOW)
    middle = jnp.where((spot == 1) | (spot == 2), 1, 0)
    flags = jnp.stack([side, middle]).astype(jnp.int32)

    groups = [g for g in range(0, length, GROUP)]

    def move(value, pairs):
        kept = [(a, b) for a, b in pairs if 0 <= a < length and 0 <= b < length]
        return lax.ppermute(value, "chain", kept)

    around = [(g + a, g + b) for g in groups for a, b in ((0, 2), (1, 0), (2, 3), (3, 1))]
    swapped = [(g + a, g + b) for g in groups for a, b in ((1, 2), (2, 1))]
    onward = [(g + a, g + b) for g in groups for a, b in ((1, GROUP), (2, 3 - GROUP))]
    two_up = [
        (g + a, g + b) for g in groups for a, b in ((0, 1), (1, GROUP), (2, 3), (3, GROUP + 2))
    ]
    two_down = [(b, a) for a, b in two_up]
    four_up = [(i, i + GROUP) for i in range(length)]
    four_down = [(b, a) for a, b in four_up]

    couplings = jnp.concatenate([lower, upper], axis=0)
    rhs = right_side[0]

    near = move(couplings, around)
    mine = move(couplings, swapped)
    near_rhs = move(rhs, around)
    mine_rhs = move(rhs, swapped)
    far = move(near, onward)
    far_rhs = move(near_rhs, onward)
    held, spread, own = run(
        couplings_kernel, 10, (pair, block, pair), flags, couplings, mine, near, couplings, far,
        scalars=1,
    )
    (current,) = run(
        injections_kernel, 3, (block,), flags, own, spread, rhs, mine_rhs, near_rhs, rhs, far_rhs,
        scalars=1,
    )

    below, above = move(held, two_up), move(held, two_down)
    below_rhs, above_rhs = move(current, two_up), move(current, two_down)
    next_held, spread = run(later_couplings_kernel, 10, (pair, block), held, below, above)
    (current,) = run(
        later_injections_kernel, 3, (block,), held, spread, current, below_rhs, above_rhs
    )
    held = next_held

    below_upper, above_lower = move(held[UPP], four_up), move(held[LOW], four_down)
    below_rhs, above_rhs = move(current, four_up), move(current, four_down)
    (spread,) = run(last_couplings_kernel, 6, (block,), held, below_upper, above_lower)
    (current,) = run(
        later_injections_kernel, 3, (block,), held, spread, current, below_rhs, above_rhs
    )
    returned = move(current, swapped)
    return jnp.where(middle == 1, returned, current)[None]


def solution(mesh):
    placed = P(("energy", "chain"), None, None, None)
    return jax.shard_map(
        functools.partial(local, mesh.shape["chain"]),
        mesh=mesh,
        in_specs=(placed,) * 3,
        out_specs=placed,
        check_vma=False,
    )
```

```python
import functools

import jax
import jax.numpy as jnp
from jax import lax
from jax.experimental import pallas as pl
from jax.experimental.pallas import tpu as pltpu
from jax.sharding import PartitionSpec as P

GROUP = 4
LOW, UPP = 0, 1


def wide(block):
    real, imag = block[0], block[1]
    return jnp.concatenate(
        [jnp.concatenate([real, -imag], axis=1), jnp.concatenate([imag, real], axis=1)], axis=0
    )


def tall(block):
    return block.reshape(block.shape[0] * block.shape[1], block.shape[2])


def product(left, right):
    return jnp.dot(left, right, preferred_element_type=jnp.float32)


def low(value):
    return value.astype(jnp.bfloat16)


def parts(stacked):
    return stacked.reshape(2, stacked.shape[0] // 2, stacked.shape[1])


def beside(*blocks):
    return jnp.concatenate(blocks, axis=1)


def inverse_less_one(coupling):
    order = coupling.shape[1]
    first = low(coupling)
    second = product(wide(parts(first)), first)
    second_low = low(second)
    pair = product(wide(parts(second_low)), beside(second_low, first))
    fourth = low(pair[:, :order])
    short = coupling + second + pair[:, order:]
    whole = short + pair[:, :order] + product(wide(parts(low(short))), fourth)
    return low(whole)


def solved(spread, raw):
    return low(raw.astype(jnp.float32) + product(wide(spread), low(raw)))


def row_couplings(letter, own, near, far, new, spread):
    order = spread.shape[1]
    other = 1 - letter
    by_near = product(wide(own(letter)), beside(tall(near(other)), tall(near(letter))))
    by_far = product(wide(own(other)), beside(tall(far(letter)), tall(far(other))))
    spread[...] = parts(inverse_less_one(by_near[:, :order] + by_far[:, :order]))
    solution_of = spread[...]
    new[letter] = parts(solved(solution_of, -by_near[:, order:]))
    new[other] = parts(solved(solution_of, -by_far[:, order:]))


def row_injections(letter, own, spread, rhs, near, far):
    raw = tall(rhs).astype(jnp.float32) - product(wide(own(letter)), tall(near))
    return parts(solved(spread[...], raw - product(wide(own(1 - letter)), tall(far))))


def picked(edge, at_edge, inside):
    return lambda place: jnp.where(edge, at_edge[place], inside[place])


def first_couplings_kernel(flags, held, crossed, core, onward, level, new, spread):
    edge = flags[1] == 1
    own = picked(edge, crossed, held)
    near = picked(edge, onward, core)
    far = picked(edge, level, crossed)
    row_couplings(flags[0], own, near, far, new, spread)


def first_injections_kernel(
    flags, held, crossed, spread, held_rhs, crossed_rhs, core_rhs, onward_rhs, level_rhs, new
):
    edge = flags[1] == 1
    own = picked(edge, crossed, held)
    rhs = jnp.where(edge, crossed_rhs[...], held_rhs[...])
    near = jnp.where(edge, onward_rhs[...], core_rhs[...])
    far = jnp.where(edge, level_rhs[...], crossed_rhs[...])
    new[...] = row_injections(flags[0], own, spread, rhs, near, far)


def later_couplings_kernel(flags, held, core, level, new, spread):
    def at(ref):
        return lambda place: ref[place]

    row_couplings(flags[2], at(held), at(core), at(level), new, spread)


def later_injections_kernel(flags, held, spread, rhs, core, level, new):
    new[...] = row_injections(
        flags[2], lambda place: held[place], spread, rhs[...], core[...], level[...]
    )


def last_couplings_kernel(held, below_upper, above_lower, spread):
    coupling = product(wide(held[LOW]), tall(below_upper[...]))
    coupling = coupling + product(wide(held[UPP]), tall(above_lower[...]))
    spread[...] = parts(inverse_less_one(coupling))


def last_injections_kernel(held, spread, rhs, below, above, new):
    new[...] = row_injections(
        LOW, lambda place: held[place], spread, rhs[...], below[...], above[...]
    )


def run(kernel, outs, *operands, scalars=0):
    return pl.pallas_call(
        kernel,
        out_shape=[jax.ShapeDtypeStruct(s, jnp.bfloat16) for s in outs],
        in_specs=[pl.BlockSpec(memory_space=pltpu.SMEM)] * scalars
        + [pl.BlockSpec(memory_space=pltpu.VMEM)] * (len(operands) - scalars),
        out_specs=[pl.BlockSpec(memory_space=pltpu.VMEM)] * len(outs),
        compiler_params=pltpu.CompilerParams(vmem_limit_bytes=24 * 1024 * 1024),
    )(*operands)


def local(length, lower, upper, right_side):
    block = lower.shape[1:]
    pair = (2,) + block
    spot = lax.axis_index("chain") % GROUP
    first_letter = jnp.where(spot < GROUP // 2, LOW, UPP)
    edge = jnp.where((spot == 0) | (spot == GROUP - 1), 1, 0)
    second_letter = jnp.where(spot % 2 == 0, LOW, UPP)
    flags = jnp.stack([first_letter, edge, second_letter]).astype(jnp.int32)

    groups = range(0, length, GROUP)

    def move(value, *pairs):
        moves = [(g + a, g + b) for g in groups for a, b in pairs]
        return lax.ppermute(
            value, "chain", [(a, b) for a, b in moves if 0 <= a < length and 0 <= b < length]
        )

    mirrored = ((0, 3), (1, 2), (2, 1), (3, 0))
    inward = ((0, 1), (3, 2))
    outward = ((1, 0), (2, 3))
    levels = ((0, -GROUP), (3, 3 + GROUP))
    in_core = ((0, 1), (1, 0), (2, 3), (3, 2))
    between = ((0, 1 + GROUP), (1, -GROUP), (2, 3 + GROUP), (3, 2 - GROUP))
    upward = tuple((i, i + GROUP) for i in range(GROUP))
    downward = tuple((i, i - GROUP) for i in range(GROUP))
    home = ((0, 3), (1, 1), (2, 2), (3, 0))

    held = jnp.concatenate([lower, upper], axis=0)
    rhs = right_side[0]

    crossed = move(held, *mirrored)
    level = move(held, *levels)
    core = move(held, *inward)
    crossed_rhs = move(rhs, *mirrored)
    level_rhs = move(rhs, *levels)
    core_rhs = move(rhs, *inward)
    onward = move(crossed, *outward)
    onward_rhs = move(crossed_rhs, *outward)
    new_held, spread = run(
        first_couplings_kernel, (pair, block), flags, held, crossed, core, onward, level, scalars=1
    )
    (rhs,) = run(
        first_injections_kernel, (block,),
        flags, held, crossed, spread, rhs, crossed_rhs, core_rhs, onward_rhs, level_rhs,
        scalars=1,
    )
    held = new_held

    core, level = move(held, *in_core), move(held, *between)
    core_rhs, level_rhs = move(rhs, *in_core), move(rhs, *between)
    new_held, spread = run(
        later_couplings_kernel, (pair, block), flags, held, core, level, scalars=1
    )
    (rhs,) = run(
        later_injections_kernel, (block,),
        flags, held, spread, rhs, core_rhs, level_rhs,
        scalars=1,
    )
    held = new_held

    below, above = move(held[UPP], *upward), move(held[LOW], *downward)
    below_rhs, above_rhs = move(rhs, *upward), move(rhs, *downward)
    (spread,) = run(last_couplings_kernel, (block,), held, below, above)
    (result,) = run(last_injections_kernel, (block,), held, spread, rhs, below_rhs, above_rhs)
    return move(result, *home)[None]


def solution(mesh):
    placed = P(("energy", "chain"), None, None, None)
    return jax.shard_map(
        functools.partial(local, mesh.shape["chain"]),
        mesh=mesh,
        in_specs=(placed,) * 3,
        out_specs=placed,
        check_vma=False,
    )
```

```python
import functools

import jax
import jax.numpy as jnp
from jax import lax
from jax.experimental import pallas as pl
from jax.experimental.pallas import tpu as pltpu
from jax.sharding import PartitionSpec as P

GROUP = 4
LOW, UPP, RHS = 0, 1, 2


def wide(block):
    real, imag = block[0], block[1]
    return jnp.concatenate(
        [jnp.concatenate([real, -imag], axis=1), jnp.concatenate([imag, real], axis=1)], axis=0
    )


def tall(block):
    return block.reshape(block.shape[0] * block.shape[1], block.shape[2])


def product(left, right):
    return jnp.dot(left, right, preferred_element_type=jnp.float32)


def low(value):
    return value.astype(jnp.bfloat16)


def parts(stacked):
    return stacked.reshape(2, stacked.shape[0] // 2, stacked.shape[1])


def beside(*blocks):
    return jnp.concatenate(blocks, axis=1)


def inverse_less_one(coupling):
    order = coupling.shape[1]
    first = low(coupling)
    second = product(wide(parts(first)), first)
    second_low = low(second)
    pair = product(wide(parts(second_low)), beside(second_low, first))
    fourth = low(pair[:, :order])
    short = coupling + second + pair[:, order:]
    whole = short + pair[:, :order] + product(wide(parts(low(short))), fourth)
    return low(whole)


def solved(spread, raw):
    return low(raw.astype(jnp.float32) + product(wide(spread), low(raw)))


def row_couplings(letter, own, near, far, new, spread):
    order = spread.shape[1]
    other = 1 - letter
    by_near = product(wide(own(letter)), beside(tall(near(other)), tall(near(letter))))
    by_far = product(wide(own(other)), beside(tall(far(letter)), tall(far(other))))
    spread[...] = parts(inverse_less_one(by_near[:, :order] + by_far[:, :order]))
    solution_of = spread[...]
    new[letter] = parts(solved(solution_of, -by_near[:, order:]))
    new[other] = parts(solved(solution_of, -by_far[:, order:]))


def row_injections(letter, own, spread, rhs, near, far):
    raw = tall(rhs).astype(jnp.float32) - product(wide(own(letter)), tall(near))
    return parts(solved(spread[...], raw - product(wide(own(1 - letter)), tall(far))))


def spot_of(length):
    return lax.axis_index("chain") % length


def near_kernel(own, near, half, half_rhs):
    order = near.shape[2]
    spot = spot_of(GROUP)
    kept = jnp.where(spot % 2 == 0, LOW, UPP)
    half[0] = own[kept]
    lead = wide(own[1 - kept])
    terms = product(lead, beside(tall(near[kept]), tall(near[1 - kept]), tall(near[RHS])))
    half[1] = parts(low(terms[:, :order]))
    half[2] = parts(low(-terms[:, order : 2 * order]))
    half_rhs[...] = parts(low(tall(own[RHS]).astype(jnp.float32) - terms[:, 2 * order :]))


def on_edge(there, here):
    spot = spot_of(GROUP)
    edge = (spot == 0) | (spot == GROUP - 1)
    return lambda place: jnp.where(edge, there[place], here[place])


def first_couplings_kernel(half_in, half_out, level, inner, new, spread):
    order = spread.shape[1]
    side = jnp.where(spot_of(GROUP) < GROUP // 2, UPP, LOW)
    half = on_edge(half_out, half_in)
    far = on_edge(level, inner)
    terms = product(wide(half(0)), beside(tall(far(1 - side)), tall(far(side))))
    spread[...] = parts(
        inverse_less_one(tall(half(1)).astype(jnp.float32) + terms[:, :order])
    )
    new[side] = parts(solved(spread[...], -terms[:, order:]))
    new[1 - side] = parts(solved(spread[...], tall(half(2))))


def first_injections_kernel(half_in, half_out, spread, rhs_in, rhs_out, level, inner, new):
    raw = tall(on_edge(rhs_out, rhs_in)(...)).astype(jnp.float32)
    lead = wide(on_edge(half_out, half_in)(0))
    raw = raw - product(lead, tall(on_edge(level, inner)(RHS)))
    new[...] = parts(solved(spread[...], raw))


def at(ref):
    return lambda place: ref[place]


def second_letter():
    return jnp.where(spot_of(GROUP) % 2 == 0, LOW, UPP)


def later_couplings_kernel(held, core, level, new, spread):
    row_couplings(second_letter(), at(held), at(core), at(level), new, spread)


def later_injections_kernel(held, spread, rhs, core, level, new):
    new[...] = row_injections(
        second_letter(), at(held), spread, rhs[...], core[...], level[...]
    )


def last_couplings_kernel(held, below_upper, above_lower, spread):
    coupling = product(wide(held[LOW]), tall(below_upper[...]))
    coupling = coupling + product(wide(held[UPP]), tall(above_lower[...]))
    spread[...] = parts(inverse_less_one(coupling))


def last_injections_kernel(held, spread, rhs, below, above, new):
    new[...] = row_injections(
        LOW, at(held), spread, rhs[...], below[...], above[...]
    )


def run(kernel, outs, *operands, weight=1):
    return pl.pallas_call(
        kernel,
        out_shape=[jax.ShapeDtypeStruct(s, jnp.bfloat16) for s in outs],
        in_specs=[pl.BlockSpec(memory_space=pltpu.VMEM)] * len(operands),
        out_specs=[pl.BlockSpec(memory_space=pltpu.VMEM)] * len(outs),
        compiler_params=pltpu.CompilerParams(vmem_limit_bytes=24 * 1024 * 1024),
        cost_estimate=pl.CostEstimate(flops=weight, bytes_accessed=1, transcendentals=0),
    )(*operands)


def local(length, lower, upper, right_side):
    block = lower.shape[1:]
    pair = (2,) + block
    groups = range(0, length, GROUP)

    def move(value, *pairs):
        moves = [(g + a, g + b) for g in groups for a, b in pairs]
        return lax.ppermute(
            value, "chain", [(a, b) for a, b in moves if 0 <= a < length and 0 <= b < length]
        )

    crossed = ((0, 3), (3, 0))
    inside = ((1, 2), (2, 1))
    levels = ((0, -GROUP), (3, 3 + GROUP))
    in_core = ((0, 1), (1, 0), (2, 3), (3, 2))
    between = ((0, 1 + GROUP), (1, -GROUP), (2, 3 + GROUP), (3, 2 - GROUP))
    upward = tuple((i, i + GROUP) for i in range(GROUP))
    downward = tuple((i, i - GROUP) for i in range(GROUP))
    home = ((0, 3), (1, 1), (2, 2), (3, 0))

    own = jnp.concatenate([lower, upper, right_side], axis=0)
    inner = move(own, *inside)
    near = move(own, *in_core)
    level = move(own, *levels)
    half, half_rhs = run(near_kernel, ((3,) + block, block), own, near)
    outer, outer_rhs = move(half, *crossed), move(half_rhs, *crossed)
    held, spread = run(first_couplings_kernel, (pair, block), half, outer, level, inner)
    (rhs,) = run(
        first_injections_kernel, (block,),
        half, outer, spread, half_rhs, outer_rhs, level, inner,
        weight=10**11,
    )

    core, level = move(held, *in_core), move(held, *between)
    core_rhs, level_rhs = move(rhs, *in_core), move(rhs, *between)
    new_held, spread = run(
        later_couplings_kernel, (pair, block), held, core, level
    )
    (rhs,) = run(
        later_injections_kernel, (block,),
        held, spread, rhs, core_rhs, level_rhs,
    )
    held = new_held

    below, above = move(held[UPP], *upward), move(held[LOW], *downward)
    below_rhs, above_rhs = move(rhs, *upward), move(rhs, *downward)
    (spread,) = run(last_couplings_kernel, (block,), held, below, above)
    (result,) = run(last_injections_kernel, (block,), held, spread, rhs, below_rhs, above_rhs)
    return move(result, *home)[None]


def solution(mesh):
    placed = P(("energy", "chain"), None, None, None)
    return jax.shard_map(
        functools.partial(local, mesh.shape["chain"]),
        mesh=mesh,
        in_specs=(placed,) * 3,
        out_specs=placed,
        check_vma=False,
    )
```

```python
import functools

import jax
import jax.numpy as jnp
from jax import lax
from jax.experimental import pallas as pl
from jax.experimental.pallas import tpu as pltpu
from jax.sharding import PartitionSpec as P

GROUP = 4
LOW, UPP, RHS = 0, 1, 2


def wide(block):
    real, imag = block[0], block[1]
    return jnp.concatenate(
        [jnp.concatenate([real, -imag], axis=1), jnp.concatenate([imag, real], axis=1)], axis=0
    )


def tall(block):
    return block.reshape(block.shape[0] * block.shape[1], block.shape[2])


def product(left, right):
    return jnp.dot(left, right, preferred_element_type=jnp.float32)


def low(value):
    return value.astype(jnp.bfloat16)


def parts(stacked):
    return stacked.reshape(2, stacked.shape[0] // 2, stacked.shape[1])


def beside(*blocks):
    return jnp.concatenate(blocks, axis=1)


def inverse_less_one(coupling):
    order = coupling.shape[1]
    first = low(coupling)
    second = product(wide(parts(first)), first)
    second_low = low(second)
    pair = product(wide(parts(second_low)), beside(second_low, first))
    fourth = low(pair[:, :order])
    short = coupling + second + pair[:, order:]
    whole = short + pair[:, :order] + product(wide(parts(low(short))), fourth)
    return low(whole)


def solved(spread, raw):
    return low(raw.astype(jnp.float32) + product(wide(spread), low(raw)))


def row_couplings(letter, own, near, far, new, spread):
    order = spread.shape[1]
    other = 1 - letter
    by_near = product(wide(own(letter)), beside(tall(near(other)), tall(near(letter))))
    by_far = product(wide(own(other)), beside(tall(far(letter)), tall(far(other))))
    spread[...] = parts(inverse_less_one(by_near[:, :order] + by_far[:, :order]))
    solution_of = spread[...]
    new[letter] = parts(solved(solution_of, -by_near[:, order:]))
    new[other] = parts(solved(solution_of, -by_far[:, order:]))


def row_injections(letter, own, spread, rhs, near, far):
    raw = tall(rhs).astype(jnp.float32) - product(wide(own(letter)), tall(near))
    return parts(solved(spread[...], raw - product(wide(own(1 - letter)), tall(far))))


def spot_of(length):
    return lax.axis_index("chain") % length


def on_edge(there, here):
    spot = spot_of(GROUP)
    edge = (spot == 1) | (spot == 2)
    return lambda place: jnp.where(edge, there[place], here[place])


def first_letter():
    return jnp.where(spot_of(GROUP) < GROUP // 2, LOW, UPP)


def pack_kernel(held, rhs, packed):
    packed[:2] = held[...]
    packed[2] = rhs[...]


def first_couplings_kernel(held, crossed, core, onward, level, new, spread):
    row_couplings(
        first_letter(),
        on_edge(crossed, core), on_edge(onward, held), on_edge(level, crossed),
        new, spread,
    )


def first_injections_kernel(
    crossed, spread, rhs, crossed_rhs, core, onward_rhs, level, new
):
    spot = spot_of(GROUP)
    edge = (spot == 1) | (spot == 2)
    own_rhs = jnp.where(edge, crossed_rhs[...], core[RHS])
    near = jnp.where(edge, onward_rhs[...], rhs[...])
    far = jnp.where(edge, level[RHS], crossed_rhs[...])
    new[...] = row_injections(
        first_letter(), on_edge(crossed, core), spread, own_rhs, near, far
    )


def at(ref):
    return lambda place: ref[place]


def second_letter():
    return jnp.where(spot_of(GROUP) % 2 == 0, UPP, LOW)


def later_couplings_kernel(held, core, level, new, spread):
    row_couplings(second_letter(), at(held), at(core), at(level), new, spread)


def later_injections_kernel(held, spread, rhs, core, level, new):
    new[...] = row_injections(
        second_letter(), at(held), spread, rhs[...], core[...], level[...]
    )


def last_couplings_kernel(held, below_upper, above_lower, spread):
    coupling = product(wide(held[LOW]), tall(below_upper[...]))
    coupling = coupling + product(wide(held[UPP]), tall(above_lower[...]))
    spread[...] = parts(inverse_less_one(coupling))


def last_injections_kernel(held, spread, rhs, below, above, new):
    new[...] = row_injections(
        LOW, at(held), spread, rhs[...], below[...], above[...]
    )


def run(kernel, outs, *operands, weight=1):
    return pl.pallas_call(
        kernel,
        out_shape=[jax.ShapeDtypeStruct(s, jnp.bfloat16) for s in outs],
        in_specs=[pl.BlockSpec(memory_space=pltpu.VMEM)] * len(operands),
        out_specs=[pl.BlockSpec(memory_space=pltpu.VMEM)] * len(outs),
        compiler_params=pltpu.CompilerParams(vmem_limit_bytes=24 * 1024 * 1024),
        cost_estimate=pl.CostEstimate(flops=weight, bytes_accessed=1, transcendentals=0),
    )(*operands)


def local(length, lower, upper, right_side):
    block = lower.shape[1:]
    pair = (2,) + block
    groups = range(0, length, GROUP)

    def move(value, *pairs):
        moves = [(g + a, g + b) for g in groups for a, b in pairs]
        return lax.ppermute(
            value, "chain", [(a, b) for a, b in moves if 0 <= a < length and 0 <= b < length]
        )

    mirrored = ((0, 2), (1, 3), (2, 0), (3, 1))
    inward = ((1, 0), (2, 3))
    outward = ((0, 1), (3, 2))
    levels = ((0, 1 - GROUP), (3, 2 + GROUP))
    in_core = ((0, 1), (1, 0), (2, 3), (3, 2))
    between = ((0, 1 - GROUP), (1, GROUP), (2, 3 - GROUP), (3, 2 + GROUP))
    upward = tuple((i, i + GROUP) for i in range(GROUP))
    downward = tuple((i, i - GROUP) for i in range(GROUP))
    home = ((0, 1), (1, 3), (2, 0), (3, 2))

    held = jnp.concatenate([lower, upper], axis=0)
    rhs = right_side[0]
    crossed = move(held, *mirrored)
    (packed,) = run(pack_kernel, ((3,) + block,), held, rhs)
    level = move(packed, *levels)
    core = move(packed, *inward)
    crossed_rhs = move(rhs, *mirrored)
    onward = move(crossed, *outward)
    onward_rhs = move(crossed_rhs, *outward)
    new_held, spread = run(
        first_couplings_kernel, (pair, block), held, crossed, core, onward, level, weight=1
    )
    (rhs,) = run(
        first_injections_kernel, (block,),
        crossed, spread, rhs, crossed_rhs, core, onward_rhs, level,
        weight=1,
    )
    held = new_held

    core, level = move(held, *in_core), move(held, *between)
    core_rhs, level_rhs = move(rhs, *in_core), move(rhs, *between)
    new_held, spread = run(
        later_couplings_kernel, (pair, block), held, core, level
    )
    (rhs,) = run(
        later_injections_kernel, (block,),
        held, spread, rhs, core_rhs, level_rhs,
    )
    held = new_held

    below, above = move(held[UPP], *upward), move(held[LOW], *downward)
    below_rhs, above_rhs = move(rhs, *upward), move(rhs, *downward)
    (spread,) = run(last_couplings_kernel, (block,), held, below, above)
    (result,) = run(last_injections_kernel, (block,), held, spread, rhs, below_rhs, above_rhs)
    return move(result, *home)[None]


def solution(mesh):
    placed = P(("energy", "chain"), None, None, None)
    return jax.shard_map(
        functools.partial(local, mesh.shape["chain"]),
        mesh=mesh,
        in_specs=(placed,) * 3,
        out_specs=placed,
        check_vma=False,
    )
```

```python
import functools

import jax
import jax.numpy as jnp
from jax import lax
from jax.experimental import pallas as pl
from jax.experimental.pallas import tpu as pltpu
from jax.sharding import PartitionSpec as P

GROUP = 4
LOW, UPP, RHS = 0, 1, 2


def wide(block):
    real, imag = block[0], block[1]
    return jnp.concatenate(
        [jnp.concatenate([real, -imag], axis=1), jnp.concatenate([imag, real], axis=1)], axis=0
    )


def tall(block):
    return block.reshape(block.shape[0] * block.shape[1], block.shape[2])


def product(left, right):
    return jnp.dot(left, right, preferred_element_type=jnp.float32)


def low(value):
    return value.astype(jnp.bfloat16)


def parts(stacked):
    return stacked.reshape(2, stacked.shape[0] // 2, stacked.shape[1])


def beside(*blocks):
    return jnp.concatenate(blocks, axis=1)


def inverse_less_one(coupling):
    order = coupling.shape[1]
    first = low(coupling)
    second = product(wide(parts(first)), first)
    second_low = low(second)
    pair = product(wide(parts(second_low)), beside(second_low, first))
    fourth = low(pair[:, :order])
    short = coupling + second + pair[:, order:]
    whole = short + pair[:, :order] + product(wide(parts(low(short))), fourth)
    return low(whole)


def solved(spread, raw):
    return low(raw.astype(jnp.float32) + product(wide(spread), low(raw)))


def row_couplings(letter, own, near, far, spread):
    order = spread.shape[1]
    other = 1 - letter
    by_near = product(wide(own(letter)), beside(tall(near(other)), tall(near(letter))))
    by_far = product(wide(own(other)), beside(tall(far(letter)), tall(far(other))))
    spread[...] = parts(inverse_less_one(by_near[:, :order] + by_far[:, :order]))
    solution_of = spread[...]
    return (
        parts(solved(solution_of, -by_near[:, order:])),
        parts(solved(solution_of, -by_far[:, order:])),
    )


def row_injections(letter, own, spread, rhs, near, far):
    raw = tall(rhs).astype(jnp.float32) - product(wide(own(letter)), tall(near))
    return parts(solved(spread[...], raw - product(wide(own(1 - letter)), tall(far))))


def spot_of(length):
    return lax.axis_index("chain") % length


def on_edge(there, here):
    spot = spot_of(GROUP)
    edge = (spot == 1) | (spot == 2)
    return lambda place: jnp.where(edge, there[place], here[place])


def first_letter():
    return jnp.where(spot_of(GROUP) < GROUP // 2, LOW, UPP)


def pack_kernel(held, rhs, packed):
    packed[:2] = held[...]
    packed[2] = rhs[...]


def first_couplings_kernel(held, crossed, core, onward, level, new, spread):
    letter = first_letter()
    new[letter], new[1 - letter] = row_couplings(
        letter, on_edge(crossed, core), on_edge(onward, held), on_edge(level, crossed), spread
    )


def first_injections_kernel(
    crossed, spread, rhs, crossed_rhs, core, onward_rhs, level, new
):
    spot = spot_of(GROUP)
    edge = (spot == 1) | (spot == 2)
    own_rhs = jnp.where(edge, crossed_rhs[...], core[RHS])
    near = jnp.where(edge, onward_rhs[...], rhs[...])
    far = jnp.where(edge, level[RHS], crossed_rhs[...])
    new[...] = row_injections(
        first_letter(), on_edge(crossed, core), spread, own_rhs, near, far
    )


def at(ref):
    return lambda place: ref[place]


def second_letter():
    return jnp.where(spot_of(GROUP) % 2 == 0, UPP, LOW)


def even_group():
    return lax.axis_index("chain") // GROUP % 2 == 0


def later_couplings_kernel(held, core, level, pairing, joining, spread):
    letter = second_letter()
    near, far = row_couplings(letter, at(held), at(core), at(level), spread)
    keep = (letter == UPP) == even_group()
    pairing[...] = jnp.where(keep, near, far)
    joining[...] = jnp.where(keep, far, near)


def later_injections_kernel(held, spread, rhs, core, level, new):
    new[...] = row_injections(
        second_letter(), at(held), spread, rhs[...], core[...], level[...]
    )


def last_couplings_kernel(pairing, joining, paired, joined, spread):
    coupling = product(wide(pairing), tall(paired[...]))
    coupling = coupling + product(wide(joining), tall(joined[...]))
    spread[...] = parts(inverse_less_one(coupling))


def last_injections_kernel(pairing, joining, spread, rhs, paired, joined, new):
    raw = tall(rhs[...]).astype(jnp.float32) - product(wide(pairing), tall(paired[...]))
    raw = raw - product(wide(joining), tall(joined[...]))
    new[...] = parts(solved(spread[...], raw))


def run(kernel, outs, *operands, weight=1):
    return pl.pallas_call(
        kernel,
        out_shape=[jax.ShapeDtypeStruct(s, jnp.bfloat16) for s in outs],
        in_specs=[pl.BlockSpec(memory_space=pltpu.VMEM)] * len(operands),
        out_specs=[pl.BlockSpec(memory_space=pltpu.VMEM)] * len(outs),
        compiler_params=pltpu.CompilerParams(vmem_limit_bytes=24 * 1024 * 1024),
        cost_estimate=pl.CostEstimate(flops=weight, bytes_accessed=1, transcendentals=0),
    )(*operands)


def local(length, lower, upper, right_side):
    block = lower.shape[1:]
    pair = (2,) + block
    groups = range(0, length, GROUP)

    def trade(value, pairs):
        return lax.ppermute(
            value, "chain", [(a, b) for a, b in pairs if 0 <= a < length and 0 <= b < length]
        )

    def move(value, *pairs):
        return trade(value, [(g + a, g + b) for g in groups for a, b in pairs])

    mirrored = ((0, 2), (1, 3), (2, 0), (3, 1))
    inward = ((1, 0), (2, 3))
    outward = ((0, 1), (3, 2))
    levels = ((0, 1 - GROUP), (3, 2 + GROUP))
    in_core = ((0, 1), (1, 0), (2, 3), (3, 2))
    between = ((0, 1 - GROUP), (1, GROUP), (2, 3 - GROUP), (3, 2 + GROUP))
    home = ((0, 1), (1, 3), (2, 0), (3, 2))

    held = jnp.concatenate([lower, upper], axis=0)
    rhs = right_side[0]
    crossed = move(held, *mirrored)
    (packed,) = run(pack_kernel, ((3,) + block,), held, rhs)
    level = move(packed, *levels)
    core = move(packed, *inward)
    crossed_rhs = move(rhs, *mirrored)
    onward = move(crossed, *outward)
    onward_rhs = move(crossed_rhs, *outward)
    new_held, spread = run(
        first_couplings_kernel, (pair, block), held, crossed, core, onward, level, weight=1
    )
    (rhs,) = run(
        first_injections_kernel, (block,),
        crossed, spread, rhs, crossed_rhs, core, onward_rhs, level,
        weight=1,
    )
    held = new_held

    core, level = move(held, *in_core), move(held, *between)
    core_rhs, level_rhs = move(rhs, *in_core), move(rhs, *between)
    pairing, joining, spread = run(later_couplings_kernel, (block,) * 3, held, core, level)
    (rhs,) = run(
        later_injections_kernel, (block,),
        held, spread, rhs, core_rhs, level_rhs,
    )

    at_joint, in_pair = (
        [
            (g * GROUP + a, (g + by) * GROUP + a)
            for g in range(length // GROUP)
            for by in ((1 if g % 2 == start else -1),)
            for a in range(GROUP)
        ]
        for start in (1, 0)
    )
    joined, joined_rhs = trade(joining, at_joint), trade(rhs, at_joint)
    paired, paired_rhs = trade(pairing, in_pair), trade(rhs, in_pair)
    (spread,) = run(last_couplings_kernel, (block,), pairing, joining, paired, joined)
    (result,) = run(
        last_injections_kernel, (block,),
        pairing, joining, spread, rhs, paired_rhs, joined_rhs,
    )
    return move(result, *home)[None]


def solution(mesh):
    placed = P(("energy", "chain"), None, None, None)
    return jax.shard_map(
        functools.partial(local, mesh.shape["chain"]),
        mesh=mesh,
        in_specs=(placed,) * 3,
        out_specs=placed,
        check_vma=False,
    )
```

```python
import functools

import jax
import jax.numpy as jnp
from jax import lax
from jax.experimental import pallas as pl
from jax.experimental.pallas import tpu as pltpu
from jax.sharding import PartitionSpec as P

GROUP = 4
LOW, UPP, RHS = 0, 1, 2


def wide(block):
    real, imag = block[0], block[1]
    return jnp.concatenate(
        [jnp.concatenate([real, -imag], axis=1), jnp.concatenate([imag, real], axis=1)], axis=0
    )


def tall(block):
    return block.reshape(block.shape[0] * block.shape[1], block.shape[2])


def product(left, right):
    return jnp.dot(left, right, preferred_element_type=jnp.float32)


def low(value):
    return value.astype(jnp.bfloat16)


def parts(stacked):
    return stacked.reshape(2, stacked.shape[0] // 2, stacked.shape[1])


def beside(*blocks):
    return jnp.concatenate(blocks, axis=1)


def inverse_less_one(coupling):
    order = coupling.shape[1]
    first = low(coupling)
    second = product(wide(parts(first)), first)
    second_low = low(second)
    pair = product(wide(parts(second_low)), beside(second_low, first))
    fourth = low(pair[:, :order])
    short = coupling + second + pair[:, order:]
    whole = short + pair[:, :order] + product(wide(parts(low(short))), fourth)
    return low(whole)


def solved(spread, raw):
    return low(raw.astype(jnp.float32) + product(wide(spread), low(raw)))


def row_couplings(letter, own, near, far, spread):
    order = spread.shape[1]
    other = 1 - letter
    by_near = product(wide(own(letter)), beside(tall(near(other)), tall(near(letter))))
    by_far = product(wide(own(other)), beside(tall(far(letter)), tall(far(other))))
    spread[...] = parts(inverse_less_one(by_near[:, :order] + by_far[:, :order]))
    solution_of = spread[...]
    return (
        parts(solved(solution_of, -by_near[:, order:])),
        parts(solved(solution_of, -by_far[:, order:])),
    )


def row_injections(letter, own, spread, rhs, near, far):
    raw = tall(rhs).astype(jnp.float32) - product(wide(own(letter)), tall(near))
    return parts(solved(spread[...], raw - product(wide(own(1 - letter)), tall(far))))


def spot_of(length):
    return lax.axis_index("chain") % length


def on_edge(there, here):
    spot = spot_of(GROUP)
    edge = (spot == 1) | (spot == 2)
    return lambda place: jnp.where(edge, there[place], here[place])


def first_letter():
    return jnp.where(spot_of(GROUP) < GROUP // 2, LOW, UPP)


def pack_kernel(held, rhs, packed):
    packed[:2] = held[...]
    packed[2] = rhs[...]


def first_couplings_kernel(held, crossed, core, onward, level, new, spread):
    letter = first_letter()
    new[letter], new[1 - letter] = row_couplings(
        letter, on_edge(crossed, core), on_edge(onward, held), on_edge(level, crossed), spread
    )


def first_injections_kernel(
    crossed, spread, rhs, crossed_rhs, core, onward_rhs, level, new
):
    spot = spot_of(GROUP)
    edge = (spot == 1) | (spot == 2)
    own_rhs = jnp.where(edge, crossed_rhs[...], core[RHS])
    near = jnp.where(edge, onward_rhs[...], rhs[...])
    far = jnp.where(edge, level[RHS], crossed_rhs[...])
    new[...] = row_injections(
        first_letter(), on_edge(crossed, core), spread, own_rhs, near, far
    )


def at(ref):
    return lambda place: ref[place]


def second_letter():
    return jnp.where(spot_of(GROUP) % 2 == 0, UPP, LOW)


def even_group():
    return lax.axis_index("chain") // GROUP % 2 == 0


def later_couplings_kernel(held, core, level, pairing, joining, spread):
    letter = second_letter()
    near, far = row_couplings(letter, at(held), at(core), at(level), spread)
    keep = (letter == UPP) == even_group()
    pairing[...] = jnp.where(keep, near, far)
    joining[...] = jnp.where(keep, far, near)


def later_injections_kernel(held, spread, rhs, core, level, left, right):
    new = row_injections(
        second_letter(), at(held), spread, rhs[...], core[...], level[...]
    )
    half = left.shape[2]
    left[...] = new[:, :, :half]
    right[...] = new[:, :, half:]


def last_couplings_kernel(pairing, joining, paired, joined, spread):
    coupling = product(wide(pairing), tall(paired[...]))
    coupling = coupling + product(wide(joining), tall(joined[...]))
    spread[...] = parts(inverse_less_one(coupling))


def last_injections_kernel(pairing, joining, spread, rhs, paired, joined, new):
    raw = tall(rhs[...]).astype(jnp.float32) - product(wide(pairing), tall(paired[...]))
    raw = raw - product(wide(joining), tall(joined[...]))
    new[...] = parts(solved(spread[...], raw))


def run(kernel, outs, *operands, weight=1):
    return pl.pallas_call(
        kernel,
        out_shape=[jax.ShapeDtypeStruct(s, jnp.bfloat16) for s in outs],
        in_specs=[pl.BlockSpec(memory_space=pltpu.VMEM)] * len(operands),
        out_specs=[pl.BlockSpec(memory_space=pltpu.VMEM)] * len(outs),
        compiler_params=pltpu.CompilerParams(vmem_limit_bytes=24 * 1024 * 1024),
        cost_estimate=pl.CostEstimate(flops=weight, bytes_accessed=1, transcendentals=0),
    )(*operands)


def local(length, lower, upper, right_side):
    block = lower.shape[1:]
    pair = (2,) + block
    groups = range(0, length, GROUP)

    def trade(value, pairs):
        return lax.ppermute(
            value, "chain", [(a, b) for a, b in pairs if 0 <= a < length and 0 <= b < length]
        )

    def move(value, *pairs):
        return trade(value, [(g + a, g + b) for g in groups for a, b in pairs])

    mirrored = ((0, 2), (1, 3), (2, 0), (3, 1))
    inward = ((1, 0), (2, 3))
    outward = ((0, 1), (3, 2))
    levels = ((0, 1 - GROUP), (3, 2 + GROUP))
    in_core = ((0, 1), (1, 0), (2, 3), (3, 2))
    between = ((0, 1 - GROUP), (1, GROUP), (2, 3 - GROUP), (3, 2 + GROUP))
    home = ((0, 1), (1, 3), (2, 0), (3, 2))

    held = jnp.concatenate([lower, upper], axis=0)
    rhs = right_side[0]
    crossed = move(held, *mirrored)
    (packed,) = run(pack_kernel, ((3,) + block,), held, rhs)
    level = move(packed, *levels)
    core = move(packed, *inward)
    crossed_rhs = move(rhs, *mirrored)
    onward = move(crossed, *outward)
    onward_rhs = move(crossed_rhs, *outward)
    new_held, spread = run(
        first_couplings_kernel, (pair, block), held, crossed, core, onward, level, weight=1
    )
    (rhs,) = run(
        first_injections_kernel, (block,),
        crossed, spread, rhs, crossed_rhs, core, onward_rhs, level,
        weight=1,
    )
    held = new_held

    core, level = move(held, *in_core), move(held, *between)
    core_rhs, level_rhs = move(rhs, *in_core), move(rhs, *between)
    pairing, joining, spread = run(later_couplings_kernel, (block,) * 3, held, core, level)
    half_block = block[:2] + (block[2] // 2,)
    halves = run(
        later_injections_kernel, (half_block,) * 2,
        held, spread, rhs, core_rhs, level_rhs,
    )

    at_joint, in_pair = (
        [
            (g * GROUP + a, (g + by) * GROUP + a)
            for g in range(length // GROUP)
            for by in ((1 if g % 2 == start else -1),)
            for a in range(GROUP)
        ]
        for start in (1, 0)
    )
    joined, paired = trade(joining, at_joint), trade(pairing, in_pair)
    arrived = [(trade(half, in_pair), trade(half, at_joint)) for half in halves]
    (spread,) = run(last_couplings_kernel, (block,), pairing, joining, paired, joined)
    results = []
    for half, (paired_half, joined_half), weight in zip(halves, arrived, (1, 1)):
        (result,) = run(
            last_injections_kernel, (half_block,),
            pairing, joining, spread, half, paired_half, joined_half,
            weight=weight,
        )
        results.append(move(result, *home))
    return jnp.concatenate(results, axis=-1)[None]


def solution(mesh):
    placed = P(("energy", "chain"), None, None, None)
    return jax.shard_map(
        functools.partial(local, mesh.shape["chain"]),
        mesh=mesh,
        in_specs=(placed,) * 3,
        out_specs=placed,
        check_vma=False,
    )
```

```python
import functools

import jax
import jax.numpy as jnp
from jax import lax
from jax.experimental import pallas as pl
from jax.experimental.pallas import tpu as pltpu
from jax.sharding import PartitionSpec as P

GROUP = 4
LOW, UPP, RHS = 0, 1, 2


def wide(block):
    real, imag = block[0], block[1]
    return jnp.concatenate(
        [jnp.concatenate([real, -imag], axis=1), jnp.concatenate([imag, real], axis=1)], axis=0
    )


def tall(block):
    return block.reshape(block.shape[0] * block.shape[1], block.shape[2])


def product(left, right):
    return jnp.dot(left, right, preferred_element_type=jnp.float32)


def low(value):
    return value.astype(jnp.bfloat16)


def parts(stacked):
    return stacked.reshape(2, stacked.shape[0] // 2, stacked.shape[1])


def beside(*blocks):
    return jnp.concatenate(blocks, axis=1)


def inverse_less_one(coupling):
    order = coupling.shape[1]
    first = low(coupling)
    second = product(wide(parts(first)), first)
    second_low = low(second)
    pair = product(wide(parts(second_low)), beside(second_low, first))
    fourth = low(pair[:, :order])
    short = coupling + second + pair[:, order:]
    whole = short + pair[:, :order] + product(wide(parts(low(short))), fourth)
    return low(whole)


def solved(spread, raw):
    return low(raw.astype(jnp.float32) + product(wide(spread), low(raw)))


def row_couplings(letter, own, near, far, spread):
    order = spread.shape[1]
    other = 1 - letter
    by_near = product(wide(own(letter)), beside(tall(near(other)), tall(near(letter))))
    by_far = product(wide(own(other)), beside(tall(far(letter)), tall(far(other))))
    spread[...] = parts(inverse_less_one(by_near[:, :order] + by_far[:, :order]))
    solution_of = spread[...]
    return (
        parts(solved(solution_of, -by_near[:, order:])),
        parts(solved(solution_of, -by_far[:, order:])),
    )


def row_injections(letter, own, spread, rhs, near, far):
    raw = tall(rhs).astype(jnp.float32) - product(wide(own(letter)), tall(near))
    return parts(solved(spread[...], raw - product(wide(own(1 - letter)), tall(far))))


def spot_of(length):
    return lax.axis_index("chain") % length


def on_edge(there, here):
    spot = spot_of(GROUP)
    edge = (spot == 1) | (spot == 2)
    return lambda place: jnp.where(edge, there[place], here[place])


def first_letter():
    return jnp.where(spot_of(GROUP) < GROUP // 2, LOW, UPP)


def pack_kernel(held, rhs, packed):
    packed[:2] = held[...]
    packed[2] = rhs[...]


def first_couplings_kernel(held, crossed, core, onward, level, new, spread):
    letter = first_letter()
    new[letter], new[1 - letter] = row_couplings(
        letter, on_edge(crossed, core), on_edge(onward, held), on_edge(level, crossed), spread
    )


def near_injections_kernel(packed, core, sent):
    letter = jnp.where(spot_of(GROUP) < GROUP // 2, UPP, LOW)
    raw = tall(packed[RHS]).astype(jnp.float32)
    sent[...] = parts(low(raw - product(wide(packed[letter]), tall(core[RHS]))))


def first_injections_kernel(crossed, spread, rhs, crossed_rhs, core, level, new):
    spot = spot_of(GROUP)
    edge = (spot == 1) | (spot == 2)
    own_rhs = jnp.where(edge, crossed_rhs[...], core[RHS])
    near = jnp.where(edge, jnp.zeros(rhs.shape, rhs.dtype), rhs[...])
    far = jnp.where(edge, level[RHS], crossed_rhs[...])
    new[...] = row_injections(
        first_letter(), on_edge(crossed, core), spread, own_rhs, near, far
    )


def at(ref):
    return lambda place: ref[place]


def second_letter():
    return jnp.where(spot_of(GROUP) % 2 == 0, UPP, LOW)


def even_group():
    return lax.axis_index("chain") // GROUP % 2 == 0


def later_couplings_kernel(held, core, level, pairing, joining, spread):
    letter = second_letter()
    near, far = row_couplings(letter, at(held), at(core), at(level), spread)
    keep = (letter == UPP) == even_group()
    pairing[...] = jnp.where(keep, near, far)
    joining[...] = jnp.where(keep, far, near)


def later_injections_kernel(held, spread, rhs, core, level, left, right):
    new = row_injections(
        second_letter(), at(held), spread, rhs[...], core[...], level[...]
    )
    half = left.shape[2]
    left[...] = new[:, :, :half]
    right[...] = new[:, :, half:]


def last_couplings_kernel(pairing, joining, paired, joined, spread):
    coupling = product(wide(pairing), tall(paired[...]))
    coupling = coupling + product(wide(joining), tall(joined[...]))
    spread[...] = parts(inverse_less_one(coupling))


def last_injections_kernel(pairing, joining, spread, rhs, paired, joined, new):
    raw = tall(rhs[...]).astype(jnp.float32) - product(wide(pairing), tall(paired[...]))
    raw = raw - product(wide(joining), tall(joined[...]))
    new[...] = parts(solved(spread[...], raw))


def run(kernel, outs, *operands, weight=1):
    return pl.pallas_call(
        kernel,
        out_shape=[jax.ShapeDtypeStruct(s, jnp.bfloat16) for s in outs],
        in_specs=[pl.BlockSpec(memory_space=pltpu.VMEM)] * len(operands),
        out_specs=[pl.BlockSpec(memory_space=pltpu.VMEM)] * len(outs),
        compiler_params=pltpu.CompilerParams(vmem_limit_bytes=24 * 1024 * 1024),
        cost_estimate=pl.CostEstimate(flops=weight, bytes_accessed=1, transcendentals=0),
    )(*operands)


def local(length, lower, upper, right_side):
    block = lower.shape[1:]
    pair = (2,) + block
    groups = range(0, length, GROUP)

    def trade(value, pairs):
        return lax.ppermute(
            value, "chain", [(a, b) for a, b in pairs if 0 <= a < length and 0 <= b < length]
        )

    def move(value, *pairs):
        return trade(value, [(g + a, g + b) for g in groups for a, b in pairs])

    mirrored = ((0, 2), (1, 3), (2, 0), (3, 1))
    inward = ((1, 0), (2, 3))
    outward = ((0, 1), (3, 2))
    levels = ((0, 1 - GROUP), (3, 2 + GROUP))
    in_core = ((0, 1), (1, 0), (2, 3), (3, 2))
    between = ((0, 1 - GROUP), (1, GROUP), (2, 3 - GROUP), (3, 2 + GROUP))
    home = ((0, 1), (1, 3), (2, 0), (3, 2))

    held = jnp.concatenate([lower, upper], axis=0)
    rhs = right_side[0]
    crossed = move(held, *mirrored)
    (packed,) = run(pack_kernel, ((3,) + block,), held, rhs)
    level = move(packed, *levels)
    core = move(packed, *inward)
    (sent_rhs,) = run(near_injections_kernel, (block,), packed, core)
    crossed_rhs = move(sent_rhs, *mirrored)
    onward = move(crossed, *outward)
    new_held, spread = run(
        first_couplings_kernel, (pair, block), held, crossed, core, onward, level, weight=1
    )
    (rhs,) = run(
        first_injections_kernel, (block,),
        crossed, spread, rhs, crossed_rhs, core, level,
        weight=10**11,
    )
    held = new_held

    core, level = move(held, *in_core), move(held, *between)
    core_rhs, level_rhs = move(rhs, *in_core), move(rhs, *between)
    pairing, joining, spread = run(later_couplings_kernel, (block,) * 3, held, core, level)
    half_block = block[:2] + (block[2] // 2,)
    halves = run(
        later_injections_kernel, (half_block,) * 2,
        held, spread, rhs, core_rhs, level_rhs,
    )

    at_joint, in_pair = (
        [
            (g * GROUP + a, (g + by) * GROUP + a)
            for g in range(length // GROUP)
            for by in ((1 if g % 2 == start else -1),)
            for a in range(GROUP)
        ]
        for start in (1, 0)
    )
    joined, paired = trade(joining, at_joint), trade(pairing, in_pair)
    arrived = [(trade(half, in_pair), trade(half, at_joint)) for half in halves]
    (spread,) = run(last_couplings_kernel, (block,), pairing, joining, paired, joined)
    results = []
    for half, (paired_half, joined_half), weight in zip(halves, arrived, (1, 1)):
        (result,) = run(
            last_injections_kernel, (half_block,),
            pairing, joining, spread, half, paired_half, joined_half,
            weight=weight,
        )
        results.append(move(result, *home))
    return jnp.concatenate(results, axis=-1)[None]


def solution(mesh):
    placed = P(("energy", "chain"), None, None, None)
    return jax.shard_map(
        functools.partial(local, mesh.shape["chain"]),
        mesh=mesh,
        in_specs=(placed,) * 3,
        out_specs=placed,
        check_vma=False,
    )
```

```python
import functools

import jax
import jax.numpy as jnp
from jax import lax
from jax.experimental import pallas as pl
from jax.experimental.pallas import tpu as pltpu
from jax.sharding import PartitionSpec as P

GROUP = 4
LOW, UPP, RHS = 0, 1, 2


def wide(block):
    real, imag = block[0], block[1]
    return jnp.concatenate(
        [jnp.concatenate([real, -imag], axis=1), jnp.concatenate([imag, real], axis=1)], axis=0
    )


def tall(block):
    return block.reshape(block.shape[0] * block.shape[1], block.shape[2])


def product(left, right):
    return jnp.dot(left, right, preferred_element_type=jnp.float32)


def low(value):
    return value.astype(jnp.bfloat16)


def parts(stacked):
    return stacked.reshape(2, stacked.shape[0] // 2, stacked.shape[1])


def beside(*blocks):
    return jnp.concatenate(blocks, axis=1)


def inverse_less_one(coupling):
    order = coupling.shape[1]
    first = low(coupling)
    second = product(wide(parts(first)), first)
    second_low = low(second)
    pair = product(wide(parts(second_low)), beside(second_low, first))
    fourth = low(pair[:, :order])
    short = coupling + second + pair[:, order:]
    whole = short + pair[:, :order] + product(wide(parts(low(short))), fourth)
    return low(whole)


def solved(spread, raw):
    return low(raw.astype(jnp.float32) + product(wide(spread), low(raw)))


def row_couplings(letter, own, near, far, spread):
    order = spread.shape[1]
    other = 1 - letter
    by_near = product(wide(own(letter)), beside(tall(near(other)), tall(near(letter))))
    by_far = product(wide(own(other)), beside(tall(far(letter)), tall(far(other))))
    spread[...] = parts(inverse_less_one(by_near[:, :order] + by_far[:, :order]))
    solution_of = spread[...]
    return (
        parts(solved(solution_of, -by_near[:, order:])),
        parts(solved(solution_of, -by_far[:, order:])),
    )


def row_injections(letter, own, spread, rhs, near, far):
    raw = tall(rhs).astype(jnp.float32) - product(wide(own(letter)), tall(near))
    return parts(solved(spread[...], raw - product(wide(own(1 - letter)), tall(far))))


def spot_of(length):
    return lax.axis_index("chain") % length


def on_edge(there, here):
    spot = spot_of(GROUP)
    edge = (spot == 1) | (spot == 2)
    return lambda place: jnp.where(edge, there[place], here[place])


def first_letter():
    return jnp.where(spot_of(GROUP) < GROUP // 2, LOW, UPP)


def pack_kernel(held, rhs, packed):
    packed[:2] = held[...]
    packed[2] = rhs[...]


def first_couplings_kernel(held, crossed, core, onward, level, new, spread):
    letter = first_letter()
    new[letter], new[1 - letter] = row_couplings(
        letter, on_edge(crossed, core), on_edge(onward, held), on_edge(level, crossed), spread
    )


def near_injections_kernel(packed, core, sent):
    letter = jnp.where(spot_of(GROUP) < GROUP // 2, UPP, LOW)
    raw = tall(packed[RHS]).astype(jnp.float32)
    sent[...] = parts(low(raw - product(wide(packed[letter]), tall(core[RHS]))))


def first_injections_kernel(crossed, spread, rhs, crossed_rhs, core, level, new):
    spot = spot_of(GROUP)
    edge = (spot == 1) | (spot == 2)
    own_rhs = jnp.where(edge, crossed_rhs[...], core[RHS])
    near = jnp.where(edge, jnp.zeros(rhs.shape, rhs.dtype), rhs[...])
    far = jnp.where(edge, level[RHS], crossed_rhs[...])
    new[...] = row_injections(
        first_letter(), on_edge(crossed, core), spread, own_rhs, near, far
    )


def at(ref):
    return lambda place: ref[place]


def second_letter():
    return jnp.where(spot_of(GROUP) % 2 == 0, UPP, LOW)


def even_group():
    return lax.axis_index("chain") // GROUP % 2 == 0


def later_couplings_kernel(held, core, level, pairing, joining, spread):
    letter = second_letter()
    near, far = row_couplings(letter, at(held), at(core), at(level), spread)
    keep = (letter == UPP) == even_group()
    pairing[...] = jnp.where(keep, near, far)
    joining[...] = jnp.where(keep, far, near)


def later_injections_kernel(held, spread, rhs, core, level, left, right):
    new = row_injections(
        second_letter(), at(held), spread, rhs[...], core[...], level[...]
    )
    half = left.shape[2]
    left[...] = new[:, :, :half]
    right[...] = new[:, :, half:]


def last_couplings_kernel(pairing, joining, paired, joined, spread):
    coupling = product(wide(pairing), tall(paired[...]))
    coupling = coupling + product(wide(joining), tall(joined[...]))
    spread[...] = parts(inverse_less_one(coupling))


def last_injections_kernel(pairing, joining, spread, rhs, joined, paired, new):
    raw = tall(rhs[...]).astype(jnp.float32) - product(wide(pairing), tall(paired[...]))
    raw = raw - product(wide(joining), tall(joined[...]))
    new[...] = parts(solved(spread[...], raw))


def run(kernel, outs, *operands, weight=1):
    return pl.pallas_call(
        kernel,
        out_shape=[jax.ShapeDtypeStruct(s, jnp.bfloat16) for s in outs],
        in_specs=[pl.BlockSpec(memory_space=pltpu.VMEM)] * len(operands),
        out_specs=[pl.BlockSpec(memory_space=pltpu.VMEM)] * len(outs),
        compiler_params=pltpu.CompilerParams(vmem_limit_bytes=24 * 1024 * 1024),
        cost_estimate=pl.CostEstimate(flops=weight, bytes_accessed=1, transcendentals=0),
    )(*operands)


def local(length, lower, upper, right_side):
    block = lower.shape[1:]
    pair = (2,) + block
    groups = range(0, length, GROUP)

    def trade(value, pairs):
        return lax.ppermute(
            value, "chain", [(a, b) for a, b in pairs if 0 <= a < length and 0 <= b < length]
        )

    def move(value, *pairs):
        return trade(value, [(g + a, g + b) for g in groups for a, b in pairs])

    mirrored = ((0, 2), (1, 3), (2, 0), (3, 1))
    inward = ((1, 0), (2, 3))
    outward = ((0, 1), (3, 2))
    levels = ((0, 1 - GROUP), (3, 2 + GROUP))
    in_core = ((0, 1), (1, 0), (2, 3), (3, 2))
    between = ((0, 1 - GROUP), (1, GROUP), (2, 3 - GROUP), (3, 2 + GROUP))
    home = ((0, 1), (1, 3), (2, 0), (3, 2))

    held = jnp.concatenate([lower, upper], axis=0)
    rhs = right_side[0]
    crossed = move(held, *mirrored)
    (packed,) = run(pack_kernel, ((3,) + block,), held, rhs)
    level = move(packed, *levels)
    core = move(packed, *inward)
    (sent_rhs,) = run(near_injections_kernel, (block,), packed, core)
    crossed_rhs = move(sent_rhs, *mirrored)
    onward = move(crossed, *outward)
    new_held, spread = run(
        first_couplings_kernel, (pair, block), held, crossed, core, onward, level, weight=1
    )
    (rhs,) = run(
        first_injections_kernel, (block,),
        crossed, spread, rhs, crossed_rhs, core, level,
        weight=10**11,
    )
    held = new_held

    core, level = move(held, *in_core), move(held, *between)
    core_rhs, level_rhs = move(rhs, *in_core), move(rhs, *between)
    pairing, joining, spread = run(later_couplings_kernel, (block,) * 3, held, core, level)
    half_block = block[:2] + (block[2] // 2,)
    halves = run(
        later_injections_kernel, (half_block,) * 2,
        held, spread, rhs, core_rhs, level_rhs,
    )

    at_joint, in_pair = (
        [
            (g * GROUP + a, (g + by) * GROUP + a)
            for g in range(length // GROUP)
            for by in ((1 if g % 2 == start else -1),)
            for a in range(GROUP)
        ]
        for start in (1, 0)
    )
    joined, paired = trade(joining, at_joint), trade(pairing, in_pair)
    arrived = [(trade(half, in_pair), trade(half, at_joint)) for half in halves]
    (spread,) = run(last_couplings_kernel, (block,), pairing, joining, paired, joined)
    results = []
    for half, (paired_half, joined_half), weight in zip(halves, arrived, (1, 1)):
        (result,) = run(
            last_injections_kernel, (half_block,),
            pairing, joining, spread, half, joined_half, paired_half,
            weight=weight,
        )
        results.append(move(result, *home))
    return jnp.concatenate(results, axis=-1)[None]


def solution(mesh):
    placed = P(("energy", "chain"), None, None, None)
    return jax.shard_map(
        functools.partial(local, mesh.shape["chain"]),
        mesh=mesh,
        in_specs=(placed,) * 3,
        out_specs=placed,
        check_vma=False,
    )
```

```python
import functools

import jax
import jax.numpy as jnp
from jax import lax
from jax.experimental import pallas as pl
from jax.experimental.pallas import tpu as pltpu
from jax.sharding import PartitionSpec as P

GROUP = 4
LOW, UPP, RHS = 0, 1, 2


def wide(block):
    real, imag = block[0], block[1]
    return jnp.concatenate(
        [jnp.concatenate([real, -imag], axis=1), jnp.concatenate([imag, real], axis=1)], axis=0
    )


def tall(block):
    return block.reshape(block.shape[0] * block.shape[1], block.shape[2])


def product(left, right):
    return jnp.dot(left, right, preferred_element_type=jnp.float32)


def low(value):
    return value.astype(jnp.bfloat16)


def parts(stacked):
    return stacked.reshape(2, stacked.shape[0] // 2, stacked.shape[1])


def beside(*blocks):
    return jnp.concatenate(blocks, axis=1)


def inverse_less_one(coupling):
    order = coupling.shape[1]
    first = low(coupling)
    second = product(wide(parts(first)), first)
    second_low = low(second)
    pair = product(wide(parts(second_low)), beside(second_low, first))
    fourth = low(pair[:, :order])
    short = coupling + second + pair[:, order:]
    whole = short + pair[:, :order] + product(wide(parts(low(short))), fourth)
    return low(whole)


def solved(spread, raw):
    return low(raw.astype(jnp.float32) + product(wide(spread), low(raw)))


def row_couplings(letter, own, near, far, spread):
    order = spread.shape[1]
    other = 1 - letter
    by_near = product(wide(own(letter)), beside(tall(near(other)), tall(near(letter))))
    by_far = product(wide(own(other)), beside(tall(far(letter)), tall(far(other))))
    spread[...] = parts(inverse_less_one(by_near[:, :order] + by_far[:, :order]))
    solution_of = spread[...]
    return (
        parts(solved(solution_of, -by_near[:, order:])),
        parts(solved(solution_of, -by_far[:, order:])),
    )


def row_injections(letter, own, spread, rhs, near, far):
    raw = tall(rhs).astype(jnp.float32) - product(wide(own(letter)), tall(near))
    return parts(solved(spread[...], raw - product(wide(own(1 - letter)), tall(far))))


def spot_of(length):
    return lax.axis_index("chain") % length


def on_edge(there, here):
    spot = spot_of(GROUP)
    edge = (spot == 1) | (spot == 2)
    return lambda place: jnp.where(edge, there[place], here[place])


def first_letter():
    return jnp.where(spot_of(GROUP) < GROUP // 2, LOW, UPP)


def pack_kernel(held, rhs, packed):
    packed[:2] = held[...]
    packed[2] = rhs[...]


def first_couplings_kernel(held, crossed, core, onward, level, new, spread):
    letter = first_letter()
    new[letter], new[1 - letter] = row_couplings(
        letter, on_edge(crossed, core), on_edge(onward, held), on_edge(level, crossed), spread
    )


def near_injections_kernel(packed, core, sent):
    letter = jnp.where(spot_of(GROUP) < GROUP // 2, UPP, LOW)
    raw = tall(packed[RHS]).astype(jnp.float32)
    sent[...] = parts(low(raw - product(wide(packed[letter]), tall(core[RHS]))))


def first_injections_kernel(crossed, spread, rhs, crossed_rhs, core, level, new):
    spot = spot_of(GROUP)
    edge = (spot == 1) | (spot == 2)
    own_rhs = jnp.where(edge, crossed_rhs[...], core[RHS])
    near = jnp.where(edge, jnp.zeros(rhs.shape, rhs.dtype), rhs[...])
    far = jnp.where(edge, level[RHS], crossed_rhs[...])
    new[...] = row_injections(
        first_letter(), on_edge(crossed, core), spread, own_rhs, near, far
    )


def at(ref):
    return lambda place: ref[place]


def second_letter():
    return jnp.where(spot_of(GROUP) % 2 == 0, UPP, LOW)


def even_group():
    return lax.axis_index("chain") // GROUP % 2 == 0


def later_couplings_kernel(held, core, level, pairing, joining, spread):
    letter = second_letter()
    near, far = row_couplings(letter, at(held), at(core), at(level), spread)
    keep = (letter == UPP) == even_group()
    pairing[...] = jnp.where(keep, near, far)
    joining[...] = jnp.where(keep, far, near)


def later_injections_kernel(held, spread, rhs, core, level, left, right):
    new = row_injections(
        second_letter(), at(held), spread, rhs[...], core[...], level[...]
    )
    half = left.shape[2]
    left[...] = new[:, :, :half]
    right[...] = new[:, :, half:]


def last_couplings_kernel(
    pairing, joining, paired, joined, left, right, pair_lead, joint_lead, base_left, base_right
):
    order = pair_lead.shape[1]
    half = left.shape[2]
    coupling = product(wide(pairing), tall(paired[...]))
    coupling = coupling + product(wide(joining), tall(joined[...]))
    own = beside(tall(pairing[...]), tall(joining[...]), tall(left[...]), tall(right[...]))
    spread = wide(parts(inverse_less_one(coupling)))
    ready = own.astype(jnp.float32) + product(spread, own)
    pair_lead[...] = parts(low(ready[:, :order]))
    joint_lead[...] = parts(low(ready[:, order : 2 * order]))
    base_left[...] = parts(ready[:, 2 * order : 2 * order + half])
    base_right[...] = parts(ready[:, 2 * order + half :])


def last_injections_kernel(pair_lead, joint_lead, base, joined, paired, new):
    raw = tall(base[...]) - product(wide(pair_lead), tall(paired[...]))
    new[...] = parts(low(raw - product(wide(joint_lead), tall(joined[...]))))


def place_kernel(first, part, *refs):
    whole, sem = refs[-2:]
    copy = pltpu.make_async_copy(
        part, whole.at[0, :, :, pl.ds(first, part.shape[2])], sem
    )
    copy.start()
    copy.wait()


def run(kernel, outs, *operands, weight=1):
    return pl.pallas_call(
        kernel,
        out_shape=[
            jax.ShapeDtypeStruct(*o) if isinstance(o[0], tuple) else jax.ShapeDtypeStruct(o, jnp.bfloat16)
            for o in outs
        ],
        in_specs=[pl.BlockSpec(memory_space=pltpu.VMEM)] * len(operands),
        out_specs=[pl.BlockSpec(memory_space=pltpu.VMEM)] * len(outs),
        compiler_params=pltpu.CompilerParams(vmem_limit_bytes=24 * 1024 * 1024),
        cost_estimate=pl.CostEstimate(flops=weight, bytes_accessed=1, transcendentals=0),
    )(*operands)


def local(length, lower, upper, right_side):
    block = lower.shape[1:]
    pair = (2,) + block
    groups = range(0, length, GROUP)

    def trade(value, pairs):
        return lax.ppermute(
            value, "chain", [(a, b) for a, b in pairs if 0 <= a < length and 0 <= b < length]
        )

    def move(value, *pairs):
        return trade(value, [(g + a, g + b) for g in groups for a, b in pairs])

    mirrored = ((0, 2), (1, 3), (2, 0), (3, 1))
    inward = ((1, 0), (2, 3))
    outward = ((0, 1), (3, 2))
    levels = ((0, 1 - GROUP), (3, 2 + GROUP))
    in_core = ((0, 1), (1, 0), (2, 3), (3, 2))
    between = ((0, 1 - GROUP), (1, GROUP), (2, 3 - GROUP), (3, 2 + GROUP))
    home = ((0, 1), (1, 3), (2, 0), (3, 2))

    held = jnp.concatenate([lower, upper], axis=0)
    rhs = right_side[0]
    crossed = move(held, *mirrored)
    (packed,) = run(pack_kernel, ((3,) + block,), held, rhs)
    level = move(packed, *levels)
    core = move(packed, *inward)
    (sent_rhs,) = run(near_injections_kernel, (block,), packed, core)
    crossed_rhs = move(sent_rhs, *mirrored)
    onward = move(crossed, *outward)
    new_held, spread = run(
        first_couplings_kernel, (pair, block), held, crossed, core, onward, level, weight=1
    )
    (rhs,) = run(
        first_injections_kernel, (block,),
        crossed, spread, rhs, crossed_rhs, core, level,
        weight=10**11,
    )
    held = new_held

    core, level = move(held, *in_core), move(held, *between)
    core_rhs, level_rhs = move(rhs, *in_core), move(rhs, *between)
    pairing, joining, spread = run(later_couplings_kernel, (block,) * 3, held, core, level)
    half_block = block[:2] + (block[2] // 2,)
    halves = run(
        later_injections_kernel, (half_block,) * 2,
        held, spread, rhs, core_rhs, level_rhs,
    )

    at_joint, in_pair = (
        [
            (g * GROUP + a, (g + by) * GROUP + a)
            for g in range(length // GROUP)
            for by in ((1 if g % 2 == start else -1),)
            for a in range(GROUP)
        ]
        for start in (1, 0)
    )
    joined, paired = trade(joining, at_joint), trade(pairing, in_pair)
    arrived = [(trade(half, in_pair), trade(half, at_joint)) for half in halves]
    pair_lead, joint_lead, *bases = run(
        last_couplings_kernel, (block,) * 2 + ((half_block, jnp.float32),) * 2,
        pairing, joining, paired, joined, *halves,
    )
    results = []
    for base, (paired_half, joined_half) in zip(bases, arrived):
        (result,) = run(
            last_injections_kernel, (half_block,),
            pair_lead, joint_lead, base, joined_half, paired_half,
        )
        results.append(move(result, *home))
    whole = ()
    for place, result in enumerate(results):
        whole = pl.pallas_call(
            functools.partial(place_kernel, place * half_block[2]),
            out_shape=[jax.ShapeDtypeStruct((1,) + block, jnp.bfloat16)],
            in_specs=[pl.BlockSpec(memory_space=pltpu.VMEM)]
            + [pl.BlockSpec(memory_space=pltpu.HBM)] * len(whole),
            out_specs=[pl.BlockSpec(memory_space=pltpu.HBM)],
            scratch_shapes=[pltpu.SemaphoreType.DMA],
            input_output_aliases={1: 0} if whole else {},
            compiler_params=pltpu.CompilerParams(vmem_limit_bytes=4 * 1024 * 1024),
        )(result, *whole)
    return whole[0]


def solution(mesh):
    placed = P(("energy", "chain"), None, None, None)
    return jax.shard_map(
        functools.partial(local, mesh.shape["chain"]),
        mesh=mesh,
        in_specs=(placed,) * 3,
        out_specs=placed,
        check_vma=False,
    )
```
